32 devices in a mesh: grp: 2 (over x), blk: 16 (over z, y, core).
Axes of the slice: x: 2, y: 2, z: 4, core: 2. Of those that a mesh axis runs over, the one named last changes fastest.
Arguments:
- left_values: bfloat16 [4096, 128], P(('grp', 'blk')), parts along dimension 0, may hold values from -6 to 6
- left_dirs: bfloat16 [4096, 128], P(('grp', 'blk')), parts along dimension 0, may hold values from -6 to 6
- left_pos: int32 [4096], P(('grp', 'blk')), parts along dimension 0, may hold values from 0 to 2047, each once
- right_dirs: bfloat16 [4096, 128], P(('grp', 'blk')), parts along dimension 0, may hold values from -0.5 to 0.5
- right_values: bfloat16 [4096, 128], P(('grp', 'blk')), parts along dimension 0, may hold values from -0.5 to 0.5
- right_pos: int32 [4096], P(('grp', 'blk')), parts along dimension 0, may hold values from 0 to 2047, each once
- sketch_seed: int32 [2], P('grp'), parts along dimension 0, may hold values from 0 to 1073741823
Outputs:
- sketch_loewner: float32 [4, 2048, 512], P('grp', 'blk'), parts along dimension 0
- sketch_shifted: float32 [4, 2048, 512], P('grp', 'blk'), parts along dimension 0
- gram_loewner: float32 [1024, 512], P('grp'), parts along dimension 0
- gram_shifted: float32 [1024, 512], P('grp'), parts along dimension 0
The draws below stay inside these ranges and needn't reach their ends.
There are 2 independent parts, one for each index of `grp`. The reference program is written for one: setup_inputs(seed, part) draws one part's arguments, and reference() takes and returns one part's arrays. A program takes and returns all parts, laid end to end along the dimension named above; each array names one. Nothing has to cross between parts.
Inputs may be any that keep to these rules, and one draw needn't show every extreme that they name: `left_pos`: each of 0 to 2047 appears exactly once. `right_pos`: each of 0 to 2047 appears exactly once.
All inputs are finite; a program needn't handle non-finite values.
Results may differ from the reference program's by a relative error of at most 0.003.
Values may be sent and summed in bfloat16 or wider, within the bound.
A program may use at most 64 MiB of HBM per device.

```python
import math
import jax
import jax.numpy as jnp
from jax import lax

PORTS = 64
SKETCH = 512
LEFT = 2048
RIGHT = 2048


def steps_of(own_key, extent, cuts, least, largest):
    level, own = 1.0, jax.random.fold_in(own_key, 6)
    for position, blocks in cuts:
        draws = jnp.exp(jax.random.uniform(jax.random.fold_in(own, position), (blocks,), jnp.float32, least / len(cuts), largest / len(cuts)))
        level = level * jnp.repeat(draws, extent[position] // blocks).reshape([-1 if axis == position else 1 for axis in range(len(extent))])
    return level


def gaussian(key, shape, width, bound, cuts=(), kind=jnp.bfloat16):
    array = width * jax.random.normal(key, shape, jnp.float32)
    if cuts:
        array = array * steps_of(key, shape, cuts, -0.22, 0.18)
    return jnp.clip(array, -bound, bound).astype(kind)


def setup_inputs(seed: int = 0, part: int = 0) -> dict:
    key_list = jax.random.split(jax.random.key(seed), 8)
    own_keys = jax.random.split(jax.random.fold_in(key_list[7], part), 8)
    left_values = gaussian(own_keys[0], (LEFT, 2 * PORTS), 1.0, 6.0, ((0, 16),))
    left_dirs = gaussian(own_keys[1], (LEFT, 2 * PORTS), 1.0, 6.0, ((0, 16),))
    left_pos = jax.random.permutation(own_keys[2], LEFT).astype(jnp.int32)
    right_dirs = gaussian(own_keys[3], (RIGHT, 2 * PORTS), (2 * PORTS) ** -0.5, 0.5, ((0, 16),))
    right_values = gaussian(own_keys[4], (RIGHT, 2 * PORTS), (2 * PORTS) ** -0.5, 0.5, ((0, 16),))
    right_pos = jax.random.permutation(own_keys[5], RIGHT).astype(jnp.int32)
    sketch_seed = jax.random.randint(own_keys[6], (1,), 0, 1073741824).astype(jnp.int32)
    return dict(left_values=left_values, left_dirs=left_dirs, left_pos=left_pos, right_dirs=right_dirs, right_values=right_values, right_pos=right_pos, sketch_seed=sketch_seed)


def sketch_block(seed_value, first_row, row_count, sketch_width):
    row_index = first_row + jnp.arange(row_count, dtype=jnp.int32)[:, None]
    col_index = jnp.arange(2 * sketch_width, dtype=jnp.int32)[None, :]
    hashed = seed_value * 374761393 + row_index * 668265263 + col_index * 1274126177
    hashed = hashed ^ ((hashed >> 15) & 131071)
    hashed = hashed * 2146121005
    hashed = hashed ^ ((hashed >> 13) & 524287)
    hashed = hashed * 1948299397
    hashed = hashed ^ ((hashed >> 16) & 65535)
    level_code = (hashed >> 8) & 255
    return ((level_code.astype(jnp.float32) - 127.5) / 128.0).astype(jnp.bfloat16)


def four_forms(matrix):
    half_width = matrix.shape[1] // 2
    real_part = matrix[:, :half_width]
    imag_part = matrix[:, half_width:]
    return jnp.concatenate([
        jnp.concatenate([real_part, -imag_part], 1),
        jnp.concatenate([imag_part, real_part], 1),
        jnp.concatenate([real_part, imag_part], 1),
        jnp.concatenate([-imag_part, real_part], 1)], 0)


def real_form(first_real, first_imag, second_real, second_imag):
    upper_row = jnp.concatenate([first_real + second_real, second_imag - first_imag], 1)
    lower_row = jnp.concatenate([first_imag + second_imag, first_real - second_real], 1)
    return upper_row, lower_row


def pencil_blocks(left_values, left_dirs, left_freq, left_hat, right_dirs, right_values, right_freq, right_hat, sketch_rows):
    row_count = left_values.shape[0]
    col_count = right_dirs.shape[0]
    sketch_width = sketch_rows.shape[1] // 2
    upper_terms = jnp.dot(left_values, four_forms(right_dirs).T, preferred_element_type=jnp.float32).reshape(row_count, 4, col_count)
    lower_terms = jnp.dot(left_dirs, four_forms(right_values).T, preferred_element_type=jnp.float32).reshape(row_count, 4, col_count)
    differ = left_freq[:, None] - right_freq[None, :]
    summed = left_freq[:, None] + right_freq[None, :]
    hat_left = left_hat[:, None]
    hat_right = right_hat[None, :]
    loewner_real = (upper_terms[:, 1] - lower_terms[:, 1]) / differ
    loewner_imag = (lower_terms[:, 0] - upper_terms[:, 0]) / differ
    mirror_real = (upper_terms[:, 3] - lower_terms[:, 3]) / summed
    mirror_imag = (lower_terms[:, 2] - upper_terms[:, 2]) / summed
    shifted_real = (hat_left * upper_terms[:, 0] - hat_right * lower_terms[:, 0]) / differ
    shifted_imag = (hat_left * upper_terms[:, 1] - hat_right * lower_terms[:, 1]) / differ
    flipped_real = (hat_left * upper_terms[:, 2] + hat_right * lower_terms[:, 2]) / summed
    flipped_imag = (hat_left * upper_terms[:, 3] + hat_right * lower_terms[:, 3]) / summed
    loewner_upper, loewner_lower = real_form(loewner_real, loewner_imag, mirror_real, mirror_imag)
    shifted_upper, shifted_lower = real_form(shifted_real, shifted_imag, flipped_real, flipped_imag)
    blocks = jnp.concatenate([loewner_upper, loewner_lower, shifted_upper, shifted_lower], 0).astype(jnp.bfloat16)
    stacked_sketch = jnp.concatenate([sketch_rows[:, :sketch_width], sketch_rows[:, sketch_width:]], 0)
    return jnp.dot(blocks, stacked_sketch, preferred_element_type=jnp.float32)


def reference(left_values, left_dirs, left_pos, right_dirs, right_values, right_pos, sketch_seed):
    left_freq = (2 * left_pos - LEFT).astype(jnp.float32) + 0.25
    right_freq = (2 * right_pos + 1 - LEFT).astype(jnp.float32) + 0.25
    left_hat = left_freq / LEFT
    right_hat = right_freq / LEFT
    sketch_rows = sketch_block(sketch_seed[0], 0, RIGHT, SKETCH)
    block_rows = math.gcd(LEFT, 256)
    block_count = LEFT // block_rows

    def one_block(pieces):
        values_piece, dirs_piece, freq_piece, hat_piece = pieces
        return pencil_blocks(values_piece, dirs_piece, freq_piece, hat_piece, right_dirs, right_values, right_freq, right_hat, sketch_rows)

    results = lax.map(one_block, (left_values.reshape(block_count, block_rows, -1), left_dirs.reshape(block_count, block_rows, -1), left_freq.reshape(block_count, block_rows), left_hat.reshape(block_count, block_rows)))
    results = results.reshape(block_count, 4, block_rows, SKETCH).transpose(1, 0, 2, 3).reshape(2, 2, LEFT, SKETCH)
    sketch_loewner = results[0]
    sketch_shifted = results[1]
    flat_loewner = sketch_loewner.reshape(2 * LEFT, SKETCH)
    flat_shifted = sketch_shifted.reshape(2 * LEFT, SKETCH)
    gram_loewner = jnp.dot(flat_loewner.T, flat_loewner, precision=lax.Precision.HIGHEST, preferred_element_type=jnp.float32) / (2 * LEFT)
    gram_shifted = jnp.dot(flat_shifted.T, flat_shifted, precision=lax.Precision.HIGHEST, preferred_element_type=jnp.float32) / (2 * LEFT)
    return (sketch_loewner, sketch_shifted, gram_loewner, gram_shifted)
```

```python
import functools

import jax
import jax.numpy as jnp
from jax import lax
from jax.experimental import pallas as pl
from jax.experimental.pallas import tpu as pltpu
from jax.sharding import PartitionSpec as P

SKETCH = 512
TILE = 128
TILES = [(p, q) for p in range(SKETCH // TILE) for q in range(p, SKETCH // TILE)]
HALF_STEP = (SKETCH * 1274126177 + 2**31) % 2**32 - 2**31
BF = jnp.bfloat16
F32 = jnp.float32


def chunk_rows_of(chips):
    per_chip = -(-len(TILES) * TILE // chips)
    return -(-per_chip // 16) * 16


def kernel(
    blk,
    lv_in, ld_in, lp_in, rd_in, rw_in, rp_in, seed,
    out, gall, mus,
    lv, ld, lp, lvp, ldp, lpp,
    gath, gpos,
    xs, fls, num, wblk, sk, acc, tacc, recv, trecv, tsend,
    zs, zrecv, gpart, yrecv, zsend, zgot,
    in_sem, pair_send, pair_recv, ring_send, ring_recv,
    pos_send, pos_recv, y_send, y_recv, z_send, z_recv,
    az_send, az_recv, ay_send, ay_recv, core_send, core_recv,
    mu_send, mu_recv,
):
    rows = lv_in.shape[0]
    chips = blk // 2
    half = chips // 2
    total = rows * blk
    me = lax.axis_index("blk")
    core = lax.rem(me, 2)
    chip = me // 2
    partner = me + 1 - 2 * core

    def device(chip_index):
        return {"blk": 2 * chip_index + core}

    row_y = lax.rem(chip, 2)
    row_z = chip // 2
    ring = (1 - 2 * row_y) * row_z + row_y * (2 * half - 1)

    def chip_at(position):
        q = lax.rem(position + 2 * chips, chips)
        y = q // half
        z = (1 - y) * q + y * (2 * half - 1 - q)
        return 2 * z + y

    own_slot = chips - 1
    ins = [
        pltpu.make_async_copy(src, dst, in_sem.at[i])
        for i, (src, dst) in enumerate((
            (rd_in, gath.at[own_slot, :, pl.ds(0, TILE)]),
            (rw_in, gath.at[own_slot, :, pl.ds(TILE, TILE)]),
            (rp_in, gpos.at[chip]),
            (lv_in, lv), (ld_in, ld), (lp_in, lp),
        ))
    ]
    for one in ins:
        one.start()

    barrier = pltpu.get_barrier_semaphore()
    pl.semaphore_signal(
        barrier, inc=1, device_id={"blk": partner}, device_id_type=pl.DeviceIdType.MESH
    )

    @pl.loop(1, chips)
    def _(o):
        pl.semaphore_signal(
            barrier, inc=1, device_id=device(lax.rem(chip + o, chips)),
            device_id_type=pl.DeviceIdType.MESH,
        )

    hr, hc = 16, 512
    base = (
        lax.broadcasted_iota(jnp.int32, (hr, hc), 0) * 668265263
        + lax.broadcasted_iota(jnp.int32, (hr, hc), 1) * 1274126177
    )
    seed_term = seed[0] * 374761393

    def hash_slot(source, pair, place):
        first = place * rows

        @pl.loop(0, rows // hr)
        def _(b):
            for side in range(2):
                j = (2 * source + core) * rows + b * hr
                x = base + (seed_term + j * 668265263 + side * HALF_STEP)
                x = x ^ lax.shift_right_logical(x, 15)
                x = x * 2146121005
                x = x ^ lax.shift_right_logical(x, 13)
                x = x * 1948299397
                code = (lax.shift_right_logical(x, 8) ^ lax.shift_right_logical(x, 24)) & 255
                row0 = pl.multiple_of(side * 2 * rows + first + b * hr, hr)
                sk[pair, pl.ds(row0, hr), :] = (code.astype(F32) - 127.5).astype(BF)

    steps = half
    hash_slot(chip, steps - 1, 1)
    acc[...] = jnp.zeros_like(acc)
    tacc[...] = jnp.zeros_like(tacc)
    for one in ins:
        one.wait()
    pl.semaphore_wait(barrier, chips)

    def copy(src, dst, send, recv_, to):
        return pltpu.make_async_remote_copy(
            src_ref=src, dst_ref=dst, send_sem=send, recv_sem=recv_,
            device_id=to, device_id_type=pl.DeviceIdType.MESH,
        )

    to_partner = {"blk": partner}
    cut = rows // 2

    def move(way, piece, t, last=False):
        first = isinstance(t, int) and t == 0
        src = own_slot if first else 2 * (t - 1) + way
        dst = 2 * t if last else 2 * t + way
        span = pl.ds(piece * cut, cut)
        return copy(
            gath.at[src, span], gath.at[dst, span],
            ring_send.at[way, piece, t], ring_recv.at[way, piece, t],
            device(chip_at(ring + 1 - 2 * way)),
        )

    ways = [(way, piece) for piece in range(2) for way in range(2)]
    for way, piece in ways:
        move(way, piece, 0).start()
    left_copies = [
        copy(lv, lvp, pair_send.at[0], pair_recv.at[0], to_partner),
        copy(ld, ldp, pair_send.at[1], pair_recv.at[1], to_partner),
        copy(lp, lpp, pair_send.at[2], pair_recv.at[2], to_partner),
    ]
    for one in left_copies:
        one.start()

    def pos_copy(o):
        return copy(gpos.at[chip], gpos.at[chip], pos_send.at[o], pos_recv.at[o],
                    device(lax.rem(chip + o, chips)))

    @pl.loop(1, chips)
    def _(o):
        pos_copy(o).start()

    lane = lax.broadcasted_iota(jnp.int32, (rows, TILE), 1)
    sub = lax.broadcasted_iota(jnp.int32, (rows, TILE), 0)
    low = lane < TILE // 2

    def left_side(side, v_ref, l_ref, p_ref):
        v = v_ref[...].astype(F32)
        l = -l_ref[...].astype(F32)
        vt = pltpu.roll(v, TILE // 2, 1)
        lt = pltpu.roll(l, TILE // 2, 1)
        for q, (a, b, keep) in enumerate(
            ((v, l, True), (vt, lt, True), (vt, lt, False), (v, l, False))
        ):
            for part, m in enumerate((a, b)):
                m = jnp.where(low, m, 0.0) if keep else jnp.where(low, 0.0, m)
                xs[side, q * rows:(q + 1) * rows, part * TILE:(part + 1) * TILE] = m.astype(BF)
        f = (2 * p_ref[...] - total).astype(F32) + 0.25
        column = jnp.sum(
            jnp.where(lane == sub, jnp.broadcast_to(f, (rows, TILE)), 0.0), axis=1, keepdims=True
        )
        fls[side] = jnp.broadcast_to(column, (rows, TILE))

    left_side(0, lv, ld, lp)
    for one in left_copies:
        one.wait()
    left_side(1, lvp, ldp, lpp)
    hash_slot(chip_at(ring - 1), 0, 0)
    hash_slot(chip_at(ring + 1), 0, 1)

    @pl.loop(1, chips)
    def _(o):
        pos_copy(o).wait()

    rb = 32

    def process(s, chip_a, chip_b):
        y = gath[pl.ds(2 * s, 2)].reshape(2 * rows, 2 * TILE)
        pos = jnp.concatenate([gpos[chip_a], gpos[chip_b]], axis=1)
        fr = (2 * pos + 1 - total).astype(F32) + 0.25
        fr = jnp.broadcast_to(fr, (rb, 2 * rows))
        for side in range(2):
            num[side] = lax.dot_general(
                xs[side], y, (((1,), (1,)), ((), ())), preferred_element_type=F32
            )
        for side in range(2):
            for b in range(rows // rb):
                r0 = b * rb
                fl1 = fls[side, r0:r0 + rb, :]
                fl = jnp.concatenate([fl1, fl1], axis=1)
                inv = 2.0 / ((fl - fr) * (fl + fr))
                al = fl * inv
                be = fr * inv
                ar = num[side, r0:r0 + rb, :]
                ai = num[side, rows + r0:rows + r0 + rb, :]
                br = num[side, 2 * rows + r0:2 * rows + r0 + rb, :]
                bi = num[side, 3 * rows + r0:3 * rows + r0 + rb, :]
                u0 = side * 2 * rows + r0
                w = 2 * rows
                wblk[u0:u0 + rb, :w] = (al * ai + be * br).astype(BF)
                wblk[u0:u0 + rb, w:] = (be * ar - al * bi).astype(BF)
                wblk[u0 + rows:u0 + rows + rb, :w] = (be * bi - al * ar).astype(BF)
                wblk[u0 + rows:u0 + rows + rb, w:] = (be * ai + al * br).astype(BF)
        acc[...] += jnp.dot(wblk[...], sk[s], preferred_element_type=F32)
        right = y[:, TILE:]
        for h in range(2):
            tacc[h] += lax.dot_general(
                right, sk[s, h * 2 * rows:(h + 1) * 2 * rows, :],
                (((0,), (0,)), ((), ())), preferred_element_type=F32,
            )

    @pl.loop(0, steps - 2)
    def _(t):
        for way, piece in ways:
            copy(gath.at[2 * t + way, pl.ds(piece * cut, cut)],
                 gath.at[2 * t + way, pl.ds(piece * cut, cut)],
                 ring_send.at[way, piece, t], ring_recv.at[way, piece, t],
                 device(chip_at(ring + 1 - 2 * way))).wait_recv()
            move(way, piece, t + 1).start()
        hash_slot(chip_at(ring - t - 2), t + 1, 0)
        hash_slot(chip_at(ring + t + 2), t + 1, 1)
        process(t, chip_at(ring - t - 1), chip_at(ring + t + 1))

    t = steps - 2
    for way, piece in ways:
        move(way, piece, t).wait_recv()
        if way == piece:
            move(way, piece, t + 1, True).start()
    hash_slot(chip_at(ring - t - 2), t + 1, 0)
    process(t, chip_at(ring - t - 1), chip_at(ring + t + 1))
    for way in range(2):
        move(way, way, t + 1, True).wait_recv()
    process(t + 1, chip_at(ring - t - 2), chip)

    tsend[...] = tacc[0, :TILE // 2] - tacc[1, TILE // 2:]
    tsums = copy(tsend, trecv, pair_send.at[4], pair_recv.at[4], to_partner)
    sums = copy(acc.at[pl.ds(2 * rows, 2 * rows)], recv, pair_send.at[3], pair_recv.at[3], to_partner)
    tsums.start()
    sums.start()
    tsums.wait_recv()
    t_all = (tsend[...] + trecv[...]) * (2.0 / (128.0 * total))
    t_high = t_all.astype(BF)
    t_low = (t_all - t_high.astype(F32)).astype(BF)
    t_stack = jnp.concatenate([t_high, t_high, t_low, t_low], axis=0)
    own_l = ld[...].astype(F32)
    hat1 = fls[0] * (1.0 / total)
    hat = jnp.concatenate([hat1] * (SKETCH // TILE), axis=1)
    l_re = jnp.where(low, own_l, 0.0).astype(BF)
    l_im = jnp.where(low, 0.0, own_l).astype(BF)
    extra_u = jnp.dot(jnp.concatenate([l_re, l_re], 1), t_stack, preferred_element_type=F32)
    extra_l = jnp.dot(jnp.concatenate([l_im, l_im], 1), t_stack, preferred_element_type=F32)
    sums.wait_recv()
    up = (acc[:rows] + recv[:rows]) * (1.0 / 128.0)
    lo = (acc[rows:2 * rows] + recv[rows:]) * (1.0 / 128.0)
    s_up = extra_u - hat * lo
    s_lo = extra_l + hat * up
    zs[0, :rows] = up.astype(BF)
    zs[0, rows:] = lo.astype(BF)
    zs[1, :rows] = s_up.astype(BF)
    zs[1, rows:] = s_lo.astype(BF)
    rows_copy = copy(zs.at[1 - core], zrecv, pair_send.at[5], pair_recv.at[5], to_partner)
    rows_copy.start()
    out[0] = up
    out[1] = lo
    out[2] = s_up
    out[3] = s_lo
    chunk = chunk_rows_of(chips)
    if chunk * chips > len(TILES) * TILE:
        pad = chunk * chips - len(TILES) * TILE
        gpart[len(TILES) * TILE:, :] = jnp.zeros((pad, TILE), BF)
    rows_copy.wait_recv()
    own = zs[core]
    other = zrecv[...]
    terms = []
    trace = jnp.zeros((1, 1), F32)
    for p in range(SKETCH // TILE):
        term = None
        for z in (own, other):
            d = lax.dot_general(
                z[:, p * TILE:(p + 1) * TILE], z[:, p * TILE:],
                (((0,), (0,)), ((), ())), preferred_element_type=F32,
            )
            term = d if term is None else term + d
        term = term * (1.0 / (2 * total))
        terms.append(term)
        diagonal = jnp.where(lane == sub, term[:, :TILE], 0.0)
        trace = trace + jnp.sum(jnp.sum(diagonal, axis=1, keepdims=True), axis=0, keepdims=True)
    mean = trace * (1.0 / SKETCH)
    mus[core, chip] = jnp.broadcast_to(mean, (1, TILE))
    at = 0
    for p in range(SKETCH // TILE):
        for q in range(SKETCH // TILE - p):
            tile = terms[p][:, q * TILE:(q + 1) * TILE]
            if q == 0:
                tile = jnp.where(lane == sub, tile - mean, tile)
            gpart[at * TILE:(at + 1) * TILE, :] = tile.astype(BF)
            at += 1

    def span_of(index):
        return pl.ds(pl.multiple_of(index * chunk, 16), chunk)

    def z_at(o):
        return lax.rem(row_z + o, half)

    neighbour = device(2 * row_z + 1 - row_y)

    def y_copy(o):
        return copy(gpart.at[span_of(2 * z_at(o) + 1 - row_y)], yrecv.at[o],
                    y_send.at[o], y_recv.at[o], neighbour)

    def z_copy(o):
        return copy(zsend.at[o], zgot.at[o], z_send.at[o], z_recv.at[o],
                    device(2 * z_at(o) + row_y))

    def mu_copy(o):
        return copy(mus.at[core, chip], mus.at[core, chip], mu_send.at[o], mu_recv.at[o],
                    device(lax.rem(chip + o, chips)))

    @pl.loop(1, half)
    def _(o):
        y_copy(o).start()

    y_copy(0).start()

    @pl.loop(1, chips)
    def _(o):
        mu_copy(o).start()

    @pl.loop(1, half)
    def _(o):
        y_copy(o).wait_recv()
        part = gpart[span_of(2 * z_at(o) + row_y), :].astype(F32) + yrecv[o].astype(F32)
        zsend[o] = part.astype(BF)
        z_copy(o).start()

    y_copy(0).wait_recv()
    share = gpart[span_of(chip), :].astype(F32) + yrecv[0].astype(F32)

    def add(o, value):
        z_copy(o).wait_recv()
        return value + zgot[o].astype(F32)

    share = lax.fori_loop(1, half, add, share)
    gall[core, span_of(chip), :] = share.astype(BF)

    def spread(o, column, send, recv_, to):
        place = span_of(2 * z_at(half - o) + column)
        return copy(gall.at[core, place], gall.at[core, place], send, recv_, to)

    def az_copy(o):
        place = span_of(chip)
        return copy(gall.at[core, place], gall.at[core, place], az_send.at[o], az_recv.at[o],
                    device(2 * z_at(o) + row_y))

    def ay_copy(o):
        return spread(o, row_y, ay_send.at[o], ay_recv.at[o], neighbour)

    def core_copy(o, other_column):
        column = 1 - row_y if other_column else row_y
        i = 1 if other_column else 0
        return spread(o, column, core_send.at[i, o], core_recv.at[i, o], to_partner)

    @pl.loop(1, half)
    def _(o):
        az_copy(o).start()

    ay_copy(0).start()
    core_copy(0, False).start()

    @pl.loop(1, chips)
    def _(o):
        mu_copy(o).wait_recv()

    mu_swap = copy(mus.at[core], mus.at[core], pair_send.at[6], pair_recv.at[6], to_partner)
    mu_swap.start()

    @pl.loop(1, half)
    def _(o):
        az_copy(o).wait_recv()
        ay_copy(o).start()
        core_copy(o, False).start()

    @pl.loop(0, half)
    def _(o):
        ay_copy(o).wait_recv()
        core_copy(o, True).start()

    @pl.loop(0, half)
    def _(o):
        core_copy(o, False).wait()
        core_copy(o, True).wait()
        ay_copy(o).wait_send()
        y_copy(o).wait_send()

    @pl.loop(1, half)
    def _(o):
        z_copy(o).wait_send()
        az_copy(o).wait_send()

    @pl.loop(1, chips)
    def _(o):
        mu_copy(o).wait_send()

    mu_swap.wait()
    for way, piece in ways:
        move(way, piece, 0).wait_send()

        @pl.loop(1, steps - 1)
        def _(t):
            move(way, piece, t).wait_send()

    for way in range(2):
        move(way, way, steps - 1, True).wait_send()
    sums.wait_send()
    tsums.wait_send()
    rows_copy.wait_send()


def finish(chips, sketches, gall, mus, out_l, out_s, gram_l, gram_s, full, sems):
    first = pltpu.make_async_copy(sketches.at[pl.ds(0, 2)], out_l, sems.at[0])
    second = pltpu.make_async_copy(sketches.at[pl.ds(2, 2)], out_s, sems.at[1])
    first.start()
    second.start()
    lane = lax.broadcasted_iota(jnp.int32, (TILE, TILE), 1)
    sub = lax.broadcasted_iota(jnp.int32, (TILE, TILE), 0)
    copies = []
    for which, out in enumerate((gram_l, gram_s)):
        mean = jnp.sum(mus[which], axis=0)
        for at, (p, q) in enumerate(TILES):
            tile = gall[which, at * TILE:(at + 1) * TILE, :].astype(F32)
            if q == p:
                tile = jnp.where(lane == sub, tile + mean, tile)
            else:
                full[which, q * TILE:(q + 1) * TILE, p * TILE:(p + 1) * TILE] = tile.T
            full[which, p * TILE:(p + 1) * TILE, q * TILE:(q + 1) * TILE] = tile
        one = pltpu.make_async_copy(full.at[which], out, sems.at[2 + which])
        one.start()
        copies.append(one)
    for one in [first, second] + copies:
        one.wait()


def solution(mesh):
    blk = mesh.shape["blk"]
    chips = blk // 2
    half = chips // 2

    def per_device(left_values, left_dirs, left_pos, right_dirs, right_values, right_pos, seed):
        rows = left_pos.shape[0]
        chunk = chunk_rows_of(chips)
        vmem = pl.BlockSpec(memory_space=pltpu.VMEM)
        hbm = pl.BlockSpec(memory_space=pltpu.HBM)
        dma = pltpu.SemaphoreType.DMA
        sketches, gall, mus = pl.pallas_call(
            functools.partial(kernel, blk),
            out_shape=(
                jax.ShapeDtypeStruct((4, rows, SKETCH), F32),
                jax.ShapeDtypeStruct((2, chunk * chips, TILE), BF),
                jax.ShapeDtypeStruct((2, chips, 1, TILE), F32),
            ),
            in_specs=[hbm] * 6 + [pl.BlockSpec(memory_space=pltpu.SMEM)],
            out_specs=(vmem,) * 3,
            scratch_shapes=[
                pltpu.VMEM((rows, TILE), BF),
                pltpu.VMEM((rows, TILE), BF),
                pltpu.VMEM((1, rows), jnp.int32),
                pltpu.VMEM((rows, TILE), BF),
                pltpu.VMEM((rows, TILE), BF),
                pltpu.VMEM((1, rows), jnp.int32),
                pltpu.VMEM((chips, rows, 2 * TILE), BF),
                pltpu.VMEM((chips, 1, rows), jnp.int32),
                pltpu.VMEM((2, 4 * rows, 2 * TILE), BF),
                pltpu.VMEM((2, rows, TILE), F32),
                pltpu.VMEM((2, 4 * rows, 2 * rows), F32),
                pltpu.VMEM((4 * rows, 4 * rows), BF),
                pltpu.VMEM((chips // 2, 4 * rows, SKETCH), BF),
                pltpu.VMEM((4 * rows, SKETCH), F32),
                pltpu.VMEM((2, TILE, SKETCH), F32),
                pltpu.VMEM((2 * rows, SKETCH), F32),
                pltpu.VMEM((TILE // 2, SKETCH), F32),
                pltpu.VMEM((TILE // 2, SKETCH), F32),
                pltpu.VMEM((2, 2 * rows, SKETCH), BF),
                pltpu.VMEM((2 * rows, SKETCH), BF),
                pltpu.VMEM((chunk * chips, TILE), BF),
                pltpu.VMEM((half, chunk, TILE), BF),
                pltpu.VMEM((half, chunk, TILE), BF),
                pltpu.VMEM((half, chunk, TILE), BF),
                dma((6,)), dma((8,)), dma((8,)),
                dma((2, 2, half)), dma((2, 2, half)),
                dma((chips,)), dma((chips,)),
                dma((half,)), dma((half,)), dma((half,)), dma((half,)),
                dma((half,)), dma((half,)), dma((half,)), dma((half,)),
                dma((2, half)), dma((2, half)),
                dma((chips,)), dma((chips,)),
            ],
            compiler_params=pltpu.CompilerParams(
                collective_id=0, has_side_effects=True, vmem_limit_bytes=48 * 1024 * 1024
            ),
        )(
            left_values, left_dirs, left_pos.reshape(1, rows),
            right_dirs, right_values, right_pos.reshape(1, rows), seed,
        )
        return pl.pallas_call(
            functools.partial(finish, chips),
            out_shape=(
                jax.ShapeDtypeStruct((2, rows, SKETCH), F32),
                jax.ShapeDtypeStruct((2, rows, SKETCH), F32),
                jax.ShapeDtypeStruct((SKETCH, SKETCH), F32),
                jax.ShapeDtypeStruct((SKETCH, SKETCH), F32),
            ),
            in_specs=[vmem] * 3,
            out_specs=(hbm,) * 4,
            scratch_shapes=[pltpu.VMEM((2, SKETCH, SKETCH), F32), dma((4,))],
            compiler_params=pltpu.CompilerParams(vmem_limit_bytes=32 * 1024 * 1024),
        )(sketches, gall, mus)

    return jax.shard_map(
        per_device,
        mesh=mesh,
        in_specs=(
            P(("grp", "blk"), None),
            P(("grp", "blk"), None),
            P(("grp", "blk")),
            P(("grp", "blk"), None),
            P(("grp", "blk"), None),
            P(("grp", "blk")),
            P("grp"),
        ),
        out_specs=(P("grp", "blk", None), P("grp", "blk", None), P("grp", None), P("grp", None)),
        check_vma=False,
    )
```

```python
import functools

import jax
import jax.numpy as jnp
from jax import lax
from jax.experimental import pallas as pl
from jax.experimental.pallas import tpu as pltpu
from jax.sharding import PartitionSpec as P

SKETCH = 512
TILE = 128
TILES = [(p, q) for p in range(SKETCH // TILE) for q in range(p, SKETCH // TILE)]
HALF_STEP = (SKETCH * 1274126177 + 2**31) % 2**32 - 2**31
BF = jnp.bfloat16
F32 = jnp.float32


def chunk_rows_of(chips):
    per_chip = -(-len(TILES) * TILE // chips)
    return -(-per_chip // 16) * 16


def kernel(
    blk,
    lv_in, ld_in, lp_in, rd_in, rw_in, rp_in, seed,
    out, gall, mus,
    lv, ld, lp, lvp, ldp, lpp,
    gath, gpos,
    xs, fls, num, wblk, sk, acc, tacc, recv, trecv, tsend,
    zs, zrecv, gpart, yrecv, zsend, zgot,
    in_sem, pair_send, pair_recv, ring_send, ring_recv,
    pos_send, pos_recv, y_send, y_recv, z_send, z_recv,
    az_send, az_recv, ay_send, ay_recv, core_send, core_recv,
    mu_send, mu_recv,
):
    rows = lv_in.shape[0]
    chips = blk // 2
    half = chips // 2
    total = rows * blk
    me = lax.axis_index("blk")
    core = lax.rem(me, 2)
    chip = me // 2
    partner = me + 1 - 2 * core

    def device(chip_index):
        return {"blk": 2 * chip_index + core}

    row_y = lax.rem(chip, 2)
    row_z = chip // 2

    def z_at(o):
        return lax.rem(row_z + o, half)

    neighbour = device(2 * row_z + 1 - row_y)

    own_slot = 0
    ins = [
        pltpu.make_async_copy(src, dst, in_sem.at[i])
        for i, (src, dst) in enumerate((
            (rd_in, gath.at[own_slot, :, pl.ds(0, TILE)]),
            (rw_in, gath.at[own_slot, :, pl.ds(TILE, TILE)]),
            (rp_in, gpos.at[chip]),
            (lv_in, lv), (ld_in, ld), (lp_in, lp),
        ))
    ]
    for one in ins:
        one.start()

    barrier = pltpu.get_barrier_semaphore()
    pl.semaphore_signal(
        barrier, inc=1, device_id={"blk": partner}, device_id_type=pl.DeviceIdType.MESH
    )

    pl.semaphore_signal(barrier, inc=1, device_id=neighbour, device_id_type=pl.DeviceIdType.MESH)

    @pl.loop(1, half)
    def _(o):
        pl.semaphore_signal(
            barrier, inc=1, device_id=device(2 * z_at(o) + row_y),
            device_id_type=pl.DeviceIdType.MESH,
        )

    hr, hc = 16, 512
    base = (
        lax.broadcasted_iota(jnp.int32, (hr, hc), 0) * 668265263
        + lax.broadcasted_iota(jnp.int32, (hr, hc), 1) * 1274126177
    )
    seed_term = seed[0] * 374761393

    def hash_slot(source, pair, place):
        first = place * rows

        @pl.loop(0, rows // hr)
        def _(b):
            for side in range(2):
                j = (2 * source + core) * rows + b * hr
                x = base + (seed_term + j * 668265263 + side * HALF_STEP)
                x = x ^ lax.shift_right_logical(x, 15)
                x = x * 2146121005
                x = x ^ lax.shift_right_logical(x, 13)
                x = x * 1948299397
                code = (lax.shift_right_logical(x, 8) ^ lax.shift_right_logical(x, 24)) & 255
                row0 = pl.multiple_of(side * 2 * rows + first + b * hr, hr)
                sk[pair, pl.ds(row0, hr), :] = (code.astype(F32) - 127.5).astype(BF)

    hash_slot(chip, 0, 0)
    acc[...] = jnp.zeros_like(acc)
    tacc[...] = jnp.zeros_like(tacc)
    for one in ins:
        one.wait()
    pl.semaphore_wait(barrier, half + 1)

    def copy(src, dst, send, recv_, to):
        return pltpu.make_async_remote_copy(
            src_ref=src, dst_ref=dst, send_sem=send, recv_sem=recv_,
            device_id=to, device_id_type=pl.DeviceIdType.MESH,
        )

    to_partner = {"blk": partner}

    def origin(o, column):
        return 2 * z_at(half - o) + column

    def along_z(o):
        return copy(gath.at[0], gath.at[2 * o], ring_send.at[0, o], ring_recv.at[0, o],
                    device(2 * z_at(o) + row_y))

    def along_y(o):
        return copy(gath.at[2 * o], gath.at[2 * o + 1], ring_send.at[1, o], ring_recv.at[1, o],
                    neighbour)

    def pos_z(o):
        return copy(gpos.at[chip], gpos.at[chip], pos_send.at[0, o], pos_recv.at[0, o],
                    device(2 * z_at(o) + row_y))

    def pos_y(o):
        place = origin(o, row_y)
        return copy(gpos.at[place], gpos.at[place], pos_send.at[1, o], pos_recv.at[1, o],
                    neighbour)

    along_y(0).start()
    pos_y(0).start()

    @pl.loop(1, half)
    def _(o):
        along_z(o).start()
        pos_z(o).start()

    left_copies = [
        copy(lv, lvp, pair_send.at[0], pair_recv.at[0], to_partner),
        copy(ld, ldp, pair_send.at[1], pair_recv.at[1], to_partner),
        copy(lp, lpp, pair_send.at[2], pair_recv.at[2], to_partner),
    ]
    for one in left_copies:
        one.start()

    lane = lax.broadcasted_iota(jnp.int32, (rows, TILE), 1)
    sub = lax.broadcasted_iota(jnp.int32, (rows, TILE), 0)
    low = lane < TILE // 2

    def left_side(side, v_ref, l_ref, p_ref):
        v = v_ref[...].astype(F32)
        l = -l_ref[...].astype(F32)
        vt = pltpu.roll(v, TILE // 2, 1)
        lt = pltpu.roll(l, TILE // 2, 1)
        for q, (a, b, keep) in enumerate(
            ((v, l, True), (vt, lt, True), (vt, lt, False), (v, l, False))
        ):
            for part, m in enumerate((a, b)):
                m = jnp.where(low, m, 0.0) if keep else jnp.where(low, 0.0, m)
                xs[side, q * rows:(q + 1) * rows, part * TILE:(part + 1) * TILE] = m.astype(BF)
        f = (2 * p_ref[...] - total).astype(F32) + 0.25
        column = jnp.sum(
            jnp.where(lane == sub, jnp.broadcast_to(f, (rows, TILE)), 0.0), axis=1, keepdims=True
        )
        fls[side] = jnp.broadcast_to(column, (rows, TILE))

    left_side(0, lv, ld, lp)
    for one in left_copies:
        one.wait()
    left_side(1, lvp, ldp, lpp)
    hash_slot(origin(0, 1 - row_y), 0, 1)

    rb = 32

    def process(s, chip_a, chip_b):
        y = gath[pl.ds(2 * s, 2)].reshape(2 * rows, 2 * TILE)
        pos = jnp.concatenate([gpos[chip_a], gpos[chip_b]], axis=1)
        fr = (2 * pos + 1 - total).astype(F32) + 0.25
        fr = jnp.broadcast_to(fr, (rb, 2 * rows))
        for side in range(2):
            num[side] = lax.dot_general(
                xs[side], y, (((1,), (1,)), ((), ())), preferred_element_type=F32
            )
        for side in range(2):
            for b in range(rows // rb):
                r0 = b * rb
                fl1 = fls[side, r0:r0 + rb, :]
                fl = jnp.concatenate([fl1, fl1], axis=1)
                inv = 2.0 / ((fl - fr) * (fl + fr))
                al = fl * inv
                be = fr * inv
                ar = num[side, r0:r0 + rb, :]
                ai = num[side, rows + r0:rows + r0 + rb, :]
                br = num[side, 2 * rows + r0:2 * rows + r0 + rb, :]
                bi = num[side, 3 * rows + r0:3 * rows + r0 + rb, :]
                u0 = side * 2 * rows + r0
                w = 2 * rows
                wblk[u0:u0 + rb, :w] = (al * ai + be * br).astype(BF)
                wblk[u0:u0 + rb, w:] = (be * ar - al * bi).astype(BF)
                wblk[u0 + rows:u0 + rows + rb, :w] = (be * bi - al * ar).astype(BF)
                wblk[u0 + rows:u0 + rows + rb, w:] = (be * ai + al * br).astype(BF)
        acc[...] += jnp.dot(wblk[...], sk[s], preferred_element_type=F32)
        right = y[:, TILE:]
        for h in range(2):
            tacc[h] += lax.dot_general(
                right, sk[s, h * 2 * rows:(h + 1) * 2 * rows, :],
                (((0,), (0,)), ((), ())), preferred_element_type=F32,
            )

    along_y(0).wait_recv()
    pos_y(0).wait_recv()
    process(0, chip, origin(0, 1 - row_y))

    @pl.loop(1, half)
    def _(o):
        hash_slot(origin(o, row_y), o, 0)
        hash_slot(origin(o, 1 - row_y), o, 1)
        along_z(o).wait_recv()
        along_y(o).start()
        pos_z(o).wait_recv()
        pos_y(o).start()

    @pl.loop(1, half)
    def _(o):
        along_y(o).wait_recv()
        pos_y(o).wait_recv()
        process(o, origin(o, row_y), origin(o, 1 - row_y))

    tsend[...] = tacc[0, :TILE // 2] - tacc[1, TILE // 2:]
    tsums = copy(tsend, trecv, pair_send.at[4], pair_recv.at[4], to_partner)
    sums = copy(acc.at[pl.ds(2 * rows, 2 * rows)], recv, pair_send.at[3], pair_recv.at[3], to_partner)
    tsums.start()
    sums.start()
    tsums.wait_recv()
    t_all = (tsend[...] + trecv[...]) * (2.0 / (128.0 * total))
    t_high = t_all.astype(BF)
    t_low = (t_all - t_high.astype(F32)).astype(BF)
    t_stack = jnp.concatenate([t_high, t_high, t_low, t_low], axis=0)
    own_l = ld[...].astype(F32)
    hat1 = fls[0] * (1.0 / total)
    hat = jnp.concatenate([hat1] * (SKETCH // TILE), axis=1)
    l_re = jnp.where(low, own_l, 0.0).astype(BF)
    l_im = jnp.where(low, 0.0, own_l).astype(BF)
    extra_u = jnp.dot(jnp.concatenate([l_re, l_re], 1), t_stack, preferred_element_type=F32)
    extra_l = jnp.dot(jnp.concatenate([l_im, l_im], 1), t_stack, preferred_element_type=F32)
    sums.wait_recv()
    up = (acc[:rows] + recv[:rows]) * (1.0 / 128.0)
    lo = (acc[rows:2 * rows] + recv[rows:]) * (1.0 / 128.0)
    s_up = extra_u - hat * lo
    s_lo = extra_l + hat * up
    zs[0, :rows] = up.astype(BF)
    zs[0, rows:] = lo.astype(BF)
    zs[1, :rows] = s_up.astype(BF)
    zs[1, rows:] = s_lo.astype(BF)
    rows_copy = copy(zs.at[1 - core], zrecv, pair_send.at[5], pair_recv.at[5], to_partner)
    rows_copy.start()
    out[0] = up
    out[1] = lo
    out[2] = s_up
    out[3] = s_lo
    chunk = chunk_rows_of(chips)
    if chunk * chips > len(TILES) * TILE:
        pad = chunk * chips - len(TILES) * TILE
        gpart[len(TILES) * TILE:, :] = jnp.zeros((pad, TILE), BF)
    rows_copy.wait_recv()
    own = zs[core]
    other = zrecv[...]
    terms = []
    trace = jnp.zeros((1, 1), F32)
    for p in range(SKETCH // TILE):
        term = None
        for z in (own, other):
            d = lax.dot_general(
                z[:, p * TILE:(p + 1) * TILE], z[:, p * TILE:],
                (((0,), (0,)), ((), ())), preferred_element_type=F32,
            )
            term = d if term is None else term + d
        term = term * (1.0 / (2 * total))
        terms.append(term)
        diagonal = jnp.where(lane == sub, term[:, :TILE], 0.0)
        trace = trace + jnp.sum(jnp.sum(diagonal, axis=1, keepdims=True), axis=0, keepdims=True)
    mean = trace * (1.0 / SKETCH)
    mus[core, chip] = jnp.broadcast_to(mean, (1, TILE))
    at = 0
    for p in range(SKETCH // TILE):
        for q in range(SKETCH // TILE - p):
            tile = terms[p][:, q * TILE:(q + 1) * TILE]
            if q == 0:
                tile = jnp.where(lane == sub, tile - mean, tile)
            gpart[at * TILE:(at + 1) * TILE, :] = tile.astype(BF)
            at += 1

    def span_of(index):
        return pl.ds(pl.multiple_of(index * chunk, 16), chunk)

    def y_copy(o):
        return copy(gpart.at[span_of(2 * z_at(o) + 1 - row_y)], yrecv.at[o],
                    y_send.at[o], y_recv.at[o], neighbour)

    def z_copy(o):
        return copy(zsend.at[o], zgot.at[o], z_send.at[o], z_recv.at[o],
                    device(2 * z_at(o) + row_y))

    def mu_z(o):
        return copy(mus.at[core, chip], mus.at[core, chip], mu_send.at[0, o], mu_recv.at[0, o],
                    device(2 * z_at(o) + row_y))

    def mu_y(o):
        place = origin(o, row_y)
        return copy(mus.at[core, place], mus.at[core, place], mu_send.at[1, o], mu_recv.at[1, o],
                    neighbour)

    @pl.loop(1, half)
    def _(o):
        y_copy(o).start()

    y_copy(0).start()

    mu_y(0).start()

    @pl.loop(1, half)
    def _(o):
        mu_z(o).start()

    @pl.loop(1, half)
    def _(o):
        y_copy(o).wait_recv()
        part = gpart[span_of(2 * z_at(o) + row_y), :].astype(F32) + yrecv[o].astype(F32)
        zsend[o] = part.astype(BF)
        z_copy(o).start()

    y_copy(0).wait_recv()
    share = gpart[span_of(chip), :].astype(F32) + yrecv[0].astype(F32)

    def add(o, value):
        z_copy(o).wait_recv()
        return value + zgot[o].astype(F32)

    share = lax.fori_loop(1, half, add, share)
    gall[core, span_of(chip), :] = share.astype(BF)

    def spread(o, column, send, recv_, to):
        place = span_of(2 * z_at(half - o) + column)
        return copy(gall.at[core, place], gall.at[core, place], send, recv_, to)

    def az_copy(o):
        place = span_of(chip)
        return copy(gall.at[core, place], gall.at[core, place], az_send.at[o], az_recv.at[o],
                    device(2 * z_at(o) + row_y))

    def ay_copy(o):
        return spread(o, row_y, ay_send.at[o], ay_recv.at[o], neighbour)

    def core_copy(o, other_column):
        column = 1 - row_y if other_column else row_y
        i = 1 if other_column else 0
        return spread(o, column, core_send.at[i, o], core_recv.at[i, o], to_partner)

    @pl.loop(1, half)
    def _(o):
        az_copy(o).start()

    ay_copy(0).start()
    core_copy(0, False).start()

    @pl.loop(1, half)
    def _(o):
        mu_z(o).wait_recv()
        mu_y(o).start()

    @pl.loop(0, half)
    def _(o):
        mu_y(o).wait_recv()

    mu_swap = copy(mus.at[core], mus.at[core], pair_send.at[6], pair_recv.at[6], to_partner)
    mu_swap.start()

    @pl.loop(1, half)
    def _(o):
        az_copy(o).wait_recv()
        ay_copy(o).start()
        core_copy(o, False).start()

    @pl.loop(0, half)
    def _(o):
        ay_copy(o).wait_recv()
        core_copy(o, True).start()

    @pl.loop(0, half)
    def _(o):
        core_copy(o, False).wait()
        core_copy(o, True).wait()
        ay_copy(o).wait_send()
        y_copy(o).wait_send()

    @pl.loop(1, half)
    def _(o):
        z_copy(o).wait_send()
        az_copy(o).wait_send()

    @pl.loop(1, half)
    def _(o):
        mu_z(o).wait_send()
        along_z(o).wait_send()
        pos_z(o).wait_send()

    @pl.loop(0, half)
    def _(o):
        mu_y(o).wait_send()
        along_y(o).wait_send()
        pos_y(o).wait_send()

    mu_swap.wait()
    sums.wait_send()
    tsums.wait_send()
    rows_copy.wait_send()


def finish(chips, sketches, gall, mus, out_l, out_s, gram_l, gram_s, full, sems):
    first = pltpu.make_async_copy(sketches.at[pl.ds(0, 2)], out_l, sems.at[0])
    second = pltpu.make_async_copy(sketches.at[pl.ds(2, 2)], out_s, sems.at[1])
    first.start()
    second.start()
    lane = lax.broadcasted_iota(jnp.int32, (TILE, TILE), 1)
    sub = lax.broadcasted_iota(jnp.int32, (TILE, TILE), 0)
    copies = []
    for which, out in enumerate((gram_l, gram_s)):
        mean = jnp.sum(mus[which], axis=0)
        for at, (p, q) in enumerate(TILES):
            tile = gall[which, at * TILE:(at + 1) * TILE, :].astype(F32)
            if q == p:
                tile = jnp.where(lane == sub, tile + mean, tile)
            else:
                full[which, q * TILE:(q + 1) * TILE, p * TILE:(p + 1) * TILE] = tile.T
            full[which, p * TILE:(p + 1) * TILE, q * TILE:(q + 1) * TILE] = tile
        one = pltpu.make_async_copy(full.at[which], out, sems.at[2 + which])
        one.start()
        copies.append(one)
    for one in [first, second] + copies:
        one.wait()


def solution(mesh):
    blk = mesh.shape["blk"]
    chips = blk // 2
    half = chips // 2

    def per_device(left_values, left_dirs, left_pos, right_dirs, right_values, right_pos, seed):
        rows = left_pos.shape[0]
        chunk = chunk_rows_of(chips)
        vmem = pl.BlockSpec(memory_space=pltpu.VMEM)
        hbm = pl.BlockSpec(memory_space=pltpu.HBM)
        dma = pltpu.SemaphoreType.DMA
        sketches, gall, mus = pl.pallas_call(
            functools.partial(kernel, blk),
            out_shape=(
                jax.ShapeDtypeStruct((4, rows, SKETCH), F32),
                jax.ShapeDtypeStruct((2, chunk * chips, TILE), BF),
                jax.ShapeDtypeStruct((2, chips, 1, TILE), F32),
            ),
            in_specs=[hbm] * 6 + [pl.BlockSpec(memory_space=pltpu.SMEM)],
            out_specs=(vmem,) * 3,
            scratch_shapes=[
                pltpu.VMEM((rows, TILE), BF),
                pltpu.VMEM((rows, TILE), BF),
                pltpu.VMEM((1, rows), jnp.int32),
                pltpu.VMEM((rows, TILE), BF),
                pltpu.VMEM((rows, TILE), BF),
                pltpu.VMEM((1, rows), jnp.int32),
                pltpu.VMEM((chips, rows, 2 * TILE), BF),
                pltpu.VMEM((chips, 1, rows), jnp.int32),
                pltpu.VMEM((2, 4 * rows, 2 * TILE), BF),
                pltpu.VMEM((2, rows, TILE), F32),
                pltpu.VMEM((2, 4 * rows, 2 * rows), F32),
                pltpu.VMEM((4 * rows, 4 * rows), BF),
                pltpu.VMEM((chips // 2, 4 * rows, SKETCH), BF),
                pltpu.VMEM((4 * rows, SKETCH), F32),
                pltpu.VMEM((2, TILE, SKETCH), F32),
                pltpu.VMEM((2 * rows, SKETCH), F32),
                pltpu.VMEM((TILE // 2, SKETCH), F32),
                pltpu.VMEM((TILE // 2, SKETCH), F32),
                pltpu.VMEM((2, 2 * rows, SKETCH), BF),
                pltpu.VMEM((2 * rows, SKETCH), BF),
                pltpu.VMEM((chunk * chips, TILE), BF),
                pltpu.VMEM((half, chunk, TILE), BF),
                pltpu.VMEM((half, chunk, TILE), BF),
                pltpu.VMEM((half, chunk, TILE), BF),
                dma((6,)), dma((8,)), dma((8,)),
                dma((2, half)), dma((2, half)),
                dma((2, half)), dma((2, half)),
                dma((half,)), dma((half,)), dma((half,)), dma((half,)),
                dma((half,)), dma((half,)), dma((half,)), dma((half,)),
                dma((2, half)), dma((2, half)),
                dma((2, half)), dma((2, half)),
            ],
            compiler_params=pltpu.CompilerParams(
                collective_id=0, has_side_effects=True, vmem_limit_bytes=48 * 1024 * 1024
            ),
        )(
            left_values, left_dirs, left_pos.reshape(1, rows),
            right_dirs, right_values, right_pos.reshape(1, rows), seed,
        )
        return pl.pallas_call(
            functools.partial(finish, chips),
            out_shape=(
                jax.ShapeDtypeStruct((2, rows, SKETCH), F32),
                jax.ShapeDtypeStruct((2, rows, SKETCH), F32),
                jax.ShapeDtypeStruct((SKETCH, SKETCH), F32),
                jax.ShapeDtypeStruct((SKETCH, SKETCH), F32),
            ),
            in_specs=[vmem] * 3,
            out_specs=(hbm,) * 4,
            scratch_shapes=[pltpu.VMEM((2, SKETCH, SKETCH), F32), dma((4,))],
            compiler_params=pltpu.CompilerParams(vmem_limit_bytes=32 * 1024 * 1024),
        )(sketches, gall, mus)

    return jax.shard_map(
        per_device,
        mesh=mesh,
        in_specs=(
            P(("grp", "blk"), None),
            P(("grp", "blk"), None),
            P(("grp", "blk")),
            P(("grp", "blk"), None),
            P(("grp", "blk"), None),
            P(("grp", "blk")),
            P("grp"),
        ),
        out_specs=(P("grp", "blk", None), P("grp", "blk", None), P("grp", None), P("grp", None)),
        check_vma=False,
    )
```
